512 devices in a mesh: ctx: 64 (over y, z), head: 8 (over x, core).
Axes of the slice: x: 4, y: 8, z: 8, core: 2. Of those that a mesh axis runs over, the one named last changes fastest.
Arguments:
- hidden_in: bfloat16 [32768, 8192], P('ctx', 'head'), may hold values from -6 to 6
- query: bfloat16 [32768, 8192], P('ctx', 'head'), may hold values from -6 to 6
- key: bfloat16 [32768, 1024], P('ctx', 'head'), may hold values from -6 to 6
- value: bfloat16 [32768, 1024], P('ctx', 'head'), may hold values from -6 to 6
- output_gradient: bfloat16 [32768, 8192], P('ctx', 'head'), may hold values from -6 to 6
- adapter_down: bfloat16 [48, 8192], P(None, 'head'), may hold values from -0.0625 to 0.0625
- up_query: bfloat16 [16, 8192], P(None, 'head'), may hold values from -0.0625 to 0.0625
- key_value_up_weight: bfloat16 [32, 1024], P(None, 'head'), may hold values from -0.1875 to 0.1875
Outputs:
- grad_query: bfloat16 [32768, 8192], P('ctx', 'head')
- key_gradient: bfloat16 [32768, 1024], P('ctx', 'head')
- value_gradient: bfloat16 [32768, 1024], P('ctx', 'head')
- grad_down: float32 [48, 8192], P(None, 'head')
- grad_up_query: float32 [16, 8192], P(None, 'head')
- grad_up_kv: float32 [32, 1024], P(None, 'head')
The draws below stay inside these ranges and needn't reach their ends.
All inputs are finite; a program needn't handle non-finite values.
Results may differ from the reference program's by a relative error of at most 0.014.
Values may be sent and summed in bfloat16 or wider, within the bound.
No kernel may reach another device: no remote copies, remote signals or barrier semaphores. Data moves between devices by JAX's collectives and lax.ppermute only.
A program may use at most 64 MiB of HBM per device.

```python
import math
import jax
import jax.numpy as jnp
from jax import lax

D = 8192
QUERY_HEADS = 64
KEY_VALUE_HEADS = 8
HEAD_WIDTH = 128
ADAPTER_RANK = 16
TOKENS_PER_INDEX = 512
SEQUENCE_TOKENS = 32768


def levels(own_key, shape, split, low, largest):
    factor_of, own = 1.0, jax.random.fold_in(own_key, 6)
    for axis_at, blocks in split:
        steps = jnp.exp(jax.random.uniform(jax.random.fold_in(own, axis_at), (blocks,), jnp.float32, low / len(split), largest / len(split)))
        factor_of = factor_of * jnp.repeat(steps, shape[axis_at] // blocks).reshape([-1 if axis == axis_at else 1 for axis in range(len(shape))])
    return factor_of


def bell_draw(key, dims, deviation, limit, split=(), kind=jnp.bfloat16):
    values = jax.random.normal(key, dims, jnp.float32) * deviation
    if len(split) > 0:
        values = levels(key, dims, split, -0.22, 0.18) * values
    return jnp.clip(values, min=-limit, max=limit).astype(kind)


def setup_inputs(seed: int = 0) -> dict:
    splits = jax.random.split(jax.random.key(seed), 9)
    hidden_in = bell_draw(splits[0], (SEQUENCE_TOKENS, D), 1.0, 6.0, ((0, 64), (1, 8)))
    query = bell_draw(splits[1], (SEQUENCE_TOKENS, QUERY_HEADS * HEAD_WIDTH), 1.0, 6.0, ((0, 64), (1, 8)))
    key = bell_draw(splits[2], (SEQUENCE_TOKENS, KEY_VALUE_HEADS * HEAD_WIDTH), 1.0, 6.0, ((0, 64), (1, 8)))
    value = bell_draw(splits[3], (SEQUENCE_TOKENS, KEY_VALUE_HEADS * HEAD_WIDTH), 1.0, 6.0, ((0, 64), (1, 8)))
    output_gradient = bell_draw(splits[4], (SEQUENCE_TOKENS, QUERY_HEADS * HEAD_WIDTH), 1.0, 6.0, ((0, 64), (1, 8)))
    adapter_down = bell_draw(splits[5], (3 * ADAPTER_RANK, D), D ** -0.5, 0.0625, ((1, 8),))
    up_query = bell_draw(splits[6], (ADAPTER_RANK, QUERY_HEADS * HEAD_WIDTH), (QUERY_HEADS * HEAD_WIDTH) ** -0.5, 0.0625, ((1, 8),))
    key_value_up_weight = bell_draw(splits[7], (2 * ADAPTER_RANK, KEY_VALUE_HEADS * HEAD_WIDTH), (KEY_VALUE_HEADS * HEAD_WIDTH) ** -0.5, 0.1875, ((1, 8),))
    return {"hidden_in": hidden_in, "query": query, "key": key, "value": value, "output_gradient": output_gradient, "adapter_down": adapter_down, "up_query": up_query, "key_value_up_weight": key_value_up_weight}


def rounded(value):
    return lax.optimization_barrier(value.astype(jnp.bfloat16)).astype(jnp.float32)

def block_states(pieces):
    rows_of_queries, gradient_rows, rows_of_keys, rows_of_values = pieces
    state_kv = jnp.einsum('sjd,sje->jde', rows_of_keys.astype(jnp.float32), rows_of_values.astype(jnp.float32))
    state_qo = jnp.einsum('tjgd,tjge->jde', rows_of_queries.astype(jnp.float32), gradient_rows.astype(jnp.float32))
    return (state_kv, state_qo)

def reference(hidden_in, query, key, value, output_gradient, adapter_down, up_query, key_value_up_weight):
    query_group_width = QUERY_HEADS // KEY_VALUE_HEADS
    number_of_blocks = SEQUENCE_TOKENS // TOKENS_PER_INDEX
    att_scale = 1.0 / math.sqrt(HEAD_WIDTH * SEQUENCE_TOKENS)
    grad_scale = 1.0 / math.sqrt(SEQUENCE_TOKENS)
    rows_of_queries = query.reshape(number_of_blocks, TOKENS_PER_INDEX, KEY_VALUE_HEADS, query_group_width, HEAD_WIDTH)
    gradient_rows = output_gradient.reshape(number_of_blocks, TOKENS_PER_INDEX, KEY_VALUE_HEADS, query_group_width, HEAD_WIDTH)
    rows_of_keys = key.reshape(number_of_blocks, TOKENS_PER_INDEX, KEY_VALUE_HEADS, HEAD_WIDTH)
    rows_of_values = value.reshape(number_of_blocks, TOKENS_PER_INDEX, KEY_VALUE_HEADS, HEAD_WIDTH)
    state_kv, state_qo = lax.map(block_states, (rows_of_queries, gradient_rows, rows_of_keys, rows_of_values))
    initial_state = jnp.zeros((1, KEY_VALUE_HEADS, HEAD_WIDTH, HEAD_WIDTH), jnp.float32)
    prefix = jnp.concatenate([initial_state, jnp.cumsum(state_kv, axis=0)[:-1]], axis=0).astype(jnp.bfloat16)
    suffix = jnp.concatenate([jnp.cumsum(state_qo[::-1], axis=0)[::-1][1:], initial_state], axis=0).astype(jnp.bfloat16)
    causal = jnp.arange(TOKENS_PER_INDEX)[None, :] <= jnp.arange(TOKENS_PER_INDEX)[:, None]

    def one_block(pieces):
        q_rows, d_rows, k_rows, v_rows, pre_state, suf_state = pieces
        q_full = q_rows.astype(jnp.float32)
        d_full = d_rows.astype(jnp.float32)
        k_full = k_rows.astype(jnp.float32)
        v_full = v_rows.astype(jnp.float32)
        pre_full = pre_state.astype(jnp.float32)
        suf_full = suf_state.astype(jnp.float32)
        score_do = rounded(jnp.where(causal, jnp.einsum('tjgd,sjd->jgts', d_full, v_full), 0.0))
        score_qk = rounded(jnp.where(causal, jnp.einsum('tjgd,sjd->jgts', q_full, k_full), 0.0))
        grad_q = jnp.einsum('jgts,sjd->tjgd', score_do, k_full) + jnp.einsum('tjge,jde->tjgd', d_full, pre_full)
        key_gradient_part = jnp.einsum('jgts,tjgd->sjd', score_do, q_full) + jnp.einsum('sje,jde->sjd', v_full, suf_full)
        value_gradient_part = jnp.einsum('jgts,tjge->sje', score_qk, d_full) + jnp.einsum('sjd,jde->sje', k_full, suf_full)
        return ((att_scale * grad_q).astype(jnp.bfloat16), (att_scale * key_gradient_part).astype(jnp.bfloat16), (att_scale * value_gradient_part).astype(jnp.bfloat16))
    grad_q, key_gradient_part, value_gradient_part = lax.map(one_block, (rows_of_queries, gradient_rows, rows_of_keys, rows_of_values, prefix, suffix))
    grad_query = grad_q.reshape(SEQUENCE_TOKENS, QUERY_HEADS * HEAD_WIDTH)
    key_gradient = key_gradient_part.reshape(SEQUENCE_TOKENS, KEY_VALUE_HEADS * HEAD_WIDTH)
    value_gradient = value_gradient_part.reshape(SEQUENCE_TOKENS, KEY_VALUE_HEADS * HEAD_WIDTH)
    low = jnp.dot(hidden_in, adapter_down.T, preferred_element_type=jnp.float32).astype(jnp.bfloat16)
    back = jnp.concatenate([jnp.dot(grad_query, up_query.T, preferred_element_type=jnp.float32), jnp.dot(key_gradient, key_value_up_weight[:ADAPTER_RANK].T, preferred_element_type=jnp.float32), jnp.dot(value_gradient, key_value_up_weight[ADAPTER_RANK:].T, preferred_element_type=jnp.float32)], axis=1).astype(jnp.bfloat16)
    grad_down = grad_scale * jnp.dot(back.T, hidden_in, preferred_element_type=jnp.float32)
    grad_up_query = grad_scale * jnp.dot(low[:, :ADAPTER_RANK].T, grad_query, preferred_element_type=jnp.float32)
    grad_up_kv = grad_scale * jnp.concatenate([jnp.dot(low[:, ADAPTER_RANK:2 * ADAPTER_RANK].T, key_gradient, preferred_element_type=jnp.float32), jnp.dot(low[:, 2 * ADAPTER_RANK:].T, value_gradient, preferred_element_type=jnp.float32)], axis=0)
    return (grad_query, key_gradient, value_gradient, grad_down, grad_up_query, grad_up_kv)
```

```python
import functools
import math

import jax
import jax.numpy as jnp
from jax import lax
from jax.experimental import pallas as pl
from jax.experimental.pallas import tpu as pltpu
from jax.sharding import Mesh
from jax.sharding import PartitionSpec as P

HEAD_WIDTH = 128
ADAPTER_RANK = 16
RINGS = 8
GRAD_ROWS = 10
MIB = 1024 * 1024
ALONE = 63

F32 = jnp.float32
BF16 = jnp.bfloat16


def params(mebibytes=16):
    return pltpu.CompilerParams(vmem_limit_bytes=mebibytes * MIB)


def nn(a, b):
    return lax.dot_general(a, b, (((1,), (0,)), ((), ())), preferred_element_type=F32)


def nt(a, b):
    return lax.dot_general(a, b, (((1,), (1,)), ((), ())), preferred_element_type=F32)


def tn(a, b):
    return lax.dot_general(a, b, (((0,), (0,)), ((), ())), preferred_element_type=F32)


def grid2(rows, columns):
    return (
        lax.broadcasted_iota(jnp.int32, (rows, columns), 0),
        lax.broadcasted_iota(jnp.int32, (rows, columns), 1),
    )


def ones_where(mask):
    return jnp.where(mask, 1.0, 0.0).astype(BF16)


def states_kernel(
    q_ref, d_ref, k_ref, v_ref, out_ref, chunk_ref, q_buf, d_buf, k_buf, v_buf, sems
):
    tokens, width = q_ref.shape
    half = tokens // 2
    copies = [
        pltpu.make_async_copy(k_ref, k_buf, sems.at[0]),
        pltpu.make_async_copy(v_ref, v_buf, sems.at[1]),
    ]
    for i in range(2):
        at = pl.ds(i * half, half)
        copies += [
            pltpu.make_async_copy(q_ref.at[at], q_buf.at[at], sems.at[2 + 2 * i]),
            pltpu.make_async_copy(d_ref.at[at], d_buf.at[at], sems.at[3 + 2 * i]),
        ]
    for copy in copies:
        copy.start()
    state_kv, state_qo = [], []
    copies[0].wait()
    copies[1].wait()
    for i in range(2):
        rows = pl.ds(i * half, half)
        state_kv.append(tn(k_buf[rows, :], v_buf[rows, :]))
    for i in range(2):
        rows = pl.ds(i * half, half)
        copies[2 + 2 * i].wait()
        copies[3 + 2 * i].wait()
        total = jnp.zeros((HEAD_WIDTH, HEAD_WIDTH), F32)
        for h in range(width // HEAD_WIDTH):
            at = pl.ds(h * HEAD_WIDTH, HEAD_WIDTH)
            total += tn(q_buf[rows, at], d_buf[rows, at])
        state_qo.append(total)
    peers, rows, _ = out_ref.shape
    rows //= 2
    whole_kv = (state_kv[0] + state_kv[1]).astype(BF16)
    whole_qo = (state_qo[0] + state_qo[1]).astype(BF16)
    for i in range(peers):
        part = slice(i * rows, (i + 1) * rows)
        out_ref[i, pl.ds(0, rows), :] = whole_kv[part]
        out_ref[i, pl.ds(rows, rows), :] = whole_qo[part]
    chunk_ref[pl.ds(0, HEAD_WIDTH), :] = state_kv[0].astype(BF16)
    chunk_ref[pl.ds(HEAD_WIDTH, HEAD_WIDTH), :] = state_qo[1].astype(BF16)


def scan_kernel(x_ref, out_ref, token_ref):
    size, rows, _ = x_ref.shape
    rows //= 2
    ring = lax.axis_index("ring")
    kv = [x_ref[i, pl.ds(0, rows), :].astype(F32) for i in range(size)]
    qo = [x_ref[i, pl.ds(rows, rows), :].astype(F32) for i in range(size)]
    nothing = jnp.zeros_like(kv[0])
    before, after = [nothing], [nothing]
    for i in range(size):
        before.append(before[-1] + kv[i])
        after.append(after[-1] + qo[size - 1 - i])
    for there in range(out_ref.shape[0] // size):
        for i in range(size):
            kv_part = jnp.where(
                ring < there, before[size], jnp.where(ring == there, before[i], nothing)
            )
            qo_part = jnp.where(
                ring > there, after[size], jnp.where(ring == there, after[size - 1 - i], nothing)
            )
            out_ref[there * size + i, pl.ds(0, rows), :] = kv_part.astype(BF16)
            out_ref[there * size + i, pl.ds(rows, rows), :] = qo_part.astype(BF16)
    token_ref[...] = jnp.zeros_like(token_ref)


def local_kernel(
    q_ref, d_ref, k_ref, v_ref, chunk_ref, after_ref, gq_ref, kg_ref, vg_ref, kv_ref
):
    tokens, width = q_ref.shape
    half = tokens // 2
    row, column = grid2(half, half)
    causal = column <= row

    def masked(scores):
        return jnp.where(causal, scores, 0.0).astype(BF16)

    kv_ref[:, pl.ds(0, HEAD_WIDTH)] = k_ref[...]
    kv_ref[:, pl.ds(HEAD_WIDTH, HEAD_WIDTH)] = v_ref[...]
    state_kv = chunk_ref[pl.ds(0, HEAD_WIDTH), :]
    state_qo = chunk_ref[pl.ds(HEAD_WIDTH, HEAD_WIDTH), :]
    for i in range(2):
        rows = pl.ds(i * half, half)
        k, v = k_ref[rows, :], v_ref[rows, :]
        if i == 0:
            key_gradient, value_gradient = nt(v, state_qo), nn(k, state_qo)
        else:
            key_gradient = value_gradient = jnp.zeros((half, HEAD_WIDTH), F32)
        for h in range(width // HEAD_WIDTH):
            at = pl.ds(h * HEAD_WIDTH, HEAD_WIDTH)
            q, d = q_ref[rows, at], d_ref[rows, at]
            score_do = masked(nt(d, v))
            score_qk = masked(nt(q, k))
            grad_query = nn(score_do, k)
            if i == 1:
                grad_query += nt(d, state_kv)
            gq_ref[rows, at] = grad_query.astype(BF16)
            key_gradient += tn(score_do, q)
            value_gradient += tn(score_qk, d)
        kg_ref[rows, :] = key_gradient
        vg_ref[rows, :] = value_gradient


def low_kernel(hidden_ref, down_ref, after_ref, out_ref):
    out_ref[...] = nt(down_ref[...], hidden_ref[...]).astype(BF16)


def grads_kernel(
    scale, state_ref, gq_ref, kgl_ref, vgl_ref, d_ref, kv_ref, up_ref, kvup_ref, low_ref,
    query_ref, key_ref, value_ref, send_ref,
):
    tokens, width = d_ref.shape
    rank = low_ref.shape[0]
    size = state_ref.shape[0] // RINGS
    state_rows = state_ref.shape[1] // 2
    prefix, suffix = [], []
    for i in range(size):
        total = sum(state_ref[ring * size + i].astype(F32) for ring in range(RINGS))
        prefix.append(total[:state_rows])
        suffix.append(total[state_rows:])
    prefix = jnp.concatenate(prefix, axis=0).astype(BF16)
    suffix = jnp.concatenate(suffix, axis=0).astype(BF16)
    k, v = kv_ref[:, pl.ds(0, HEAD_WIDTH)], kv_ref[:, pl.ds(HEAD_WIDTH, HEAD_WIDTH)]
    key_gradient = (scale * (kgl_ref[...] + nt(v, suffix))).astype(BF16)
    value_gradient = (scale * (vgl_ref[...] + nn(k, suffix))).astype(BF16)
    key_ref[...] = key_gradient
    value_ref[...] = value_gradient
    back = jnp.zeros((ADAPTER_RANK, tokens), F32)
    for h in range(width // HEAD_WIDTH):
        at = pl.ds(h * HEAD_WIDTH, HEAD_WIDTH)
        grad_query = gq_ref[:, at].astype(F32) + nt(d_ref[:, at], prefix)
        grad_query = (scale * grad_query).astype(BF16)
        query_ref[:, at] = grad_query
        back += nt(up_ref[:, at], grad_query)
    whole = jnp.concatenate(
        [
            back,
            nt(kvup_ref[pl.ds(0, ADAPTER_RANK), :], key_gradient),
            nt(kvup_ref[pl.ds(ADAPTER_RANK, ADAPTER_RANK), :], value_gradient),
        ],
        axis=0,
    ).astype(BF16)
    for i in range(send_ref.shape[0]):
        send_ref[i, pl.ds(0, rank), :] = whole
        send_ref[i, pl.ds(rank, rank), :] = low_ref[...]


def down_kernel(parts_ref, hidden_ref, query_ref, key_ref, value_ref, out_ref):
    peers, rows, _ = parts_ref.shape
    rank = rows // 2
    heads = hidden_ref.shape[1] // HEAD_WIDTH
    both = sum(parts_ref[i].astype(F32) for i in range(peers)).astype(BF16)
    back, low = both[:rank], both[rank:]
    down = nn(back, hidden_ref[...]).astype(BF16)
    up_query = nn(low[:ADAPTER_RANK], query_ref[...]).astype(BF16)
    at = heads * rank
    for i in range(heads):
        part = slice(i * HEAD_WIDTH, (i + 1) * HEAD_WIDTH)
        out_ref[pl.ds(i * rank, rank), :] = down[:, part]
        out_ref[pl.ds(at + i * ADAPTER_RANK, ADAPTER_RANK), :] = up_query[:, part]
    at += heads * ADAPTER_RANK
    out_ref[pl.ds(at, ADAPTER_RANK), :] = nn(
        low[ADAPTER_RANK : 2 * ADAPTER_RANK], key_ref[...]
    ).astype(BF16)
    at += ADAPTER_RANK
    out_ref[pl.ds(at, ADAPTER_RANK), :] = nn(
        low[2 * ADAPTER_RANK :], value_ref[...]
    ).astype(BF16)
    at += ADAPTER_RANK
    out_ref[pl.ds(at, out_ref.shape[0] - at), :] = jnp.zeros(
        (out_ref.shape[0] - at, HEAD_WIDTH), BF16
    )


def sum_kernel(x_ref, out_ref):
    rows = x_ref.shape[0]
    row, column = grid2(16, rows)
    total = nn(ones_where(lax.rem(column, GRAD_ROWS) == row), x_ref[...]).astype(BF16)
    row, column = grid2(rows, 16)
    out_ref[...] = nn(ones_where(lax.rem(row, GRAD_ROWS) == column), total).astype(BF16)


def finish_kernel(scale, x_ref, down_ref, query_ref, kv_ref):
    rank = down_ref.shape[0]
    parts = down_ref.shape[1] // HEAD_WIDTH
    for i in range(parts):
        at = pl.ds(i * HEAD_WIDTH, HEAD_WIDTH)
        down_ref[:, at] = scale * x_ref[pl.ds(i * rank, rank), :].astype(F32)
    start = parts * rank
    for i in range(parts):
        at = pl.ds(i * HEAD_WIDTH, HEAD_WIDTH)
        query_ref[:, at] = scale * x_ref[
            pl.ds(start + i * ADAPTER_RANK, ADAPTER_RANK), :
        ].astype(F32)
    start += parts * ADAPTER_RANK
    kv_ref[...] = scale * x_ref[pl.ds(start, 2 * ADAPTER_RANK), :].astype(F32)


def shape(dims, dtype):
    return jax.ShapeDtypeStruct(dims, dtype)


def call(kernel, out_shape, flops, nbytes, name, mebibytes=16, **more):
    return pl.pallas_call(
        kernel,
        out_shape=out_shape,
        compiler_params=params(mebibytes),
        cost_estimate=pl.CostEstimate(flops=flops, bytes_accessed=nbytes, transcendentals=0),
        name=name,
        **more,
    )


def exchange(blocks, axis):
    return lax.all_to_all(blocks, axis, split_axis=0, concat_axis=0, tiled=True)


def on_device(hidden, query, key, value, d_out, down, up_query, kv_up):
    tokens, width = query.shape
    heads = width // HEAD_WIDTH
    ctx_axes = ("ring", "place")
    ctx, size, peers = (lax.axis_size(axis) for axis in (ctx_axes, "place", "head"))
    ranks = down.shape[0]
    att_scale = 1.0 / math.sqrt(HEAD_WIDTH * tokens * ctx)
    grad_scale = 1.0 / math.sqrt(tokens * ctx)
    state_rows = 2 * HEAD_WIDTH // size

    block = (tokens, HEAD_WIDTH)
    hbm = pl.BlockSpec(memory_space=pltpu.HBM)
    sent, chunk = pl.pallas_call(
        states_kernel,
        in_specs=[hbm] * 4,
        out_shape=[
            shape((size, state_rows, HEAD_WIDTH), BF16),
            shape((2 * HEAD_WIDTH, HEAD_WIDTH), BF16),
        ],
        scratch_shapes=[
            pltpu.VMEM((tokens, width), BF16),
            pltpu.VMEM((tokens, width), BF16),
            pltpu.VMEM(block, BF16),
            pltpu.VMEM(block, BF16),
            pltpu.SemaphoreType.DMA((6,)),
        ],
        compiler_params=params(ALONE),
        cost_estimate=pl.CostEstimate(
            flops=10**8, bytes_accessed=2 * 10**6, transcendentals=0
        ),
        name="states",
    )(query, d_out, key, value)
    ring_states = exchange(sent, "place")

    vmem, anywhere = (pl.BlockSpec(memory_space=space) for space in (pltpu.VMEM, pl.ANY))
    low = call(
        low_kernel,
        shape((ranks, tokens), BF16),
        10**8,
        2 * 10**6,
        "low",
        ALONE,
        in_specs=[vmem, vmem, anywhere],
    )(hidden, down, chunk)

    scanned, token = call(
        scan_kernel,
        [shape((ctx, state_rows, HEAD_WIDTH), BF16), shape((8, HEAD_WIDTH), F32)],
        10**6,
        6 * 10**5,
        "scan",
    )(ring_states)
    around = exchange(scanned, ctx_axes)
    local_q, local_k, local_v, key_value = call(
        local_kernel,
        [
            shape((tokens, width), BF16),
            shape(block, F32),
            shape(block, F32),
            shape((tokens, 2 * HEAD_WIDTH), BF16),
        ],
        2 * 10**9,
        5 * 10**6,
        "local",
    )(query, d_out, key, value, chunk, token)

    grad_query, key_gradient, value_gradient, copies = call(
        functools.partial(grads_kernel, att_scale),
        [
            shape((tokens, width), BF16),
            shape(block, BF16),
            shape(block, BF16),
            shape((peers, 2 * ranks, tokens), BF16),
        ],
        2 * 10**8,
        5 * 10**6,
        "grads",
    )(
        around, local_q, local_k, local_v, d_out, key_value, up_query, kv_up, low
    )
    both_parts = exchange(copies, "head")
    rows = ctx * GRAD_ROWS
    partial = call(down_kernel, shape((rows, HEAD_WIDTH), BF16), 5 * 10**7, 2 * 10**6, "down")(
        both_parts, hidden, grad_query, key_gradient, value_gradient
    )
    split = (ctx, GRAD_ROWS // 2, 2, HEAD_WIDTH)
    gathered = exchange(partial.reshape(split), ctx_axes)
    sums = call(sum_kernel, shape((rows, HEAD_WIDTH), BF16), 10**7, 3 * 10**5, "sum")(
        gathered.reshape(rows, HEAD_WIDTH)
    )
    result = exchange(sums.reshape(split), ctx_axes)
    grad_down, grad_up_query, grad_up_kv = call(
        functools.partial(finish_kernel, grad_scale),
        [
            shape((ranks, width), F32),
            shape((ADAPTER_RANK, width), F32),
            shape((2 * ADAPTER_RANK, HEAD_WIDTH), F32),
        ],
        10**6,
        5 * 10**5,
        "finish",
    )(result.reshape(rows, HEAD_WIDTH))
    return grad_query, key_gradient, value_gradient, grad_down, grad_up_query, grad_up_kv


def solution(mesh):
    ctx, peers = mesh.devices.shape
    by_ring = Mesh(
        mesh.devices.reshape(RINGS, ctx // RINGS, peers), ("ring", "place", "head")
    )
    both = P(("ring", "place"), "head")
    over_head = P(None, "head")
    return jax.shard_map(
        on_device,
        mesh=by_ring,
        in_specs=(both,) * 5 + (over_head,) * 3,
        out_specs=(both,) * 3 + (over_head,) * 3,
        check_vma=False,
    )
```

```python
import functools
import math

import jax
import jax.numpy as jnp
from jax import lax
from jax.experimental import pallas as pl
from jax.experimental.pallas import tpu as pltpu
from jax.sharding import Mesh
from jax.sharding import PartitionSpec as P

HEAD_WIDTH = 128
ADAPTER_RANK = 16
RINGS = 8
GRAD_ROWS = 10
MIB = 1024 * 1024
ALONE = 63

F32 = jnp.float32
BF16 = jnp.bfloat16


def params(mebibytes=16):
    return pltpu.CompilerParams(vmem_limit_bytes=mebibytes * MIB)


def nn(a, b):
    return lax.dot_general(a, b, (((1,), (0,)), ((), ())), preferred_element_type=F32)


def nt(a, b):
    return lax.dot_general(a, b, (((1,), (1,)), ((), ())), preferred_element_type=F32)


def tn(a, b):
    return lax.dot_general(a, b, (((0,), (0,)), ((), ())), preferred_element_type=F32)


def grid2(rows, columns):
    return (
        lax.broadcasted_iota(jnp.int32, (rows, columns), 0),
        lax.broadcasted_iota(jnp.int32, (rows, columns), 1),
    )


def ones_where(mask):
    return jnp.where(mask, 1.0, 0.0).astype(BF16)


def states_kernel(
    q_ref, d_ref, k_ref, v_ref, out_ref, chunk_ref, q_buf, d_buf, k_buf, v_buf, sems
):
    tokens, width = q_ref.shape
    half = tokens // 2
    copies = [
        pltpu.make_async_copy(k_ref, k_buf, sems.at[0]),
        pltpu.make_async_copy(v_ref, v_buf, sems.at[1]),
    ]
    for i in range(2):
        at = pl.ds(i * half, half)
        copies += [
            pltpu.make_async_copy(q_ref.at[at], q_buf.at[at], sems.at[2 + 2 * i]),
            pltpu.make_async_copy(d_ref.at[at], d_buf.at[at], sems.at[3 + 2 * i]),
        ]
    for copy in copies:
        copy.start()
    state_kv, state_qo = [], []
    copies[0].wait()
    copies[1].wait()
    for i in range(2):
        rows = pl.ds(i * half, half)
        state_kv.append(tn(k_buf[rows, :], v_buf[rows, :]))
    for i in range(2):
        rows = pl.ds(i * half, half)
        copies[2 + 2 * i].wait()
        copies[3 + 2 * i].wait()
        total = jnp.zeros((HEAD_WIDTH, HEAD_WIDTH), F32)
        for h in range(width // HEAD_WIDTH):
            at = pl.ds(h * HEAD_WIDTH, HEAD_WIDTH)
            total += tn(q_buf[rows, at], d_buf[rows, at])
        state_qo.append(total)
    peers, rows, _ = out_ref.shape
    rows //= 2
    whole_kv = (state_kv[0] + state_kv[1]).astype(BF16)
    whole_qo = (state_qo[0] + state_qo[1]).astype(BF16)
    for i in range(peers):
        part = slice(i * rows, (i + 1) * rows)
        out_ref[i, pl.ds(0, rows), :] = whole_kv[part]
        out_ref[i, pl.ds(rows, rows), :] = whole_qo[part]
    chunk_ref[pl.ds(0, HEAD_WIDTH), :] = state_kv[0].astype(BF16)
    chunk_ref[pl.ds(HEAD_WIDTH, HEAD_WIDTH), :] = state_qo[1].astype(BF16)


def ring_kernel(x_ref, chunk_ref, after_ref, out_ref, chunk_out_ref):
    size, rows, _ = x_ref.shape
    rows //= 2
    ring = lax.axis_index("ring")
    total = sum(x_ref[i].astype(F32) for i in range(size))
    for there in range(out_ref.shape[0]):
        out_ref[there] = jnp.where(ring < there, total[:rows], total[rows:]).astype(BF16)
    chunk_out_ref[...] = chunk_ref[...]


def scan_kernel(x_ref, rings_ref, after_ref, out_ref):
    size, rows, _ = x_ref.shape
    rows //= 2
    ring = lax.axis_index("ring")
    before = jnp.zeros((rows, HEAD_WIDTH), F32)
    after = jnp.zeros((rows, HEAD_WIDTH), F32)
    for there in range(rings_ref.shape[0]):
        part = rings_ref[there].astype(F32)
        before += jnp.where(there < ring, part, 0.0)
        after += jnp.where(there > ring, part, 0.0)
    for i in range(size):
        last = size - 1 - i
        out_ref[i, pl.ds(0, rows), :] = before.astype(BF16)
        out_ref[last, pl.ds(rows, rows), :] = after.astype(BF16)
        before += x_ref[i, pl.ds(0, rows), :].astype(F32)
        after += x_ref[last, pl.ds(rows, rows), :].astype(F32)


def local_kernel(q_ref, d_ref, k_ref, v_ref, chunk_ref, gq_ref, near_ref):
    tokens, width = q_ref.shape
    half = tokens // 2
    row, column = grid2(half, half)
    causal = column <= row

    def masked(scores):
        return jnp.where(causal, scores, 0.0).astype(BF16)

    state_kv = chunk_ref[pl.ds(0, HEAD_WIDTH), :]
    state_qo = chunk_ref[pl.ds(HEAD_WIDTH, HEAD_WIDTH), :]
    for i in range(2):
        rows = pl.ds(i * half, half)
        k, v = k_ref[rows, :], v_ref[rows, :]
        if i == 0:
            key_gradient, value_gradient = nt(v, state_qo), nn(k, state_qo)
        else:
            key_gradient = value_gradient = jnp.zeros((half, HEAD_WIDTH), F32)
        for h in range(width // HEAD_WIDTH):
            at = pl.ds(h * HEAD_WIDTH, HEAD_WIDTH)
            q, d = q_ref[rows, at], d_ref[rows, at]
            score_do = masked(nt(d, v))
            score_qk = masked(nt(q, k))
            grad_query = nn(score_do, k)
            if i == 1:
                grad_query += nt(d, state_kv)
            gq_ref[rows, at] = grad_query.astype(BF16)
            key_gradient += tn(score_do, q)
            value_gradient += tn(score_qk, d)
        both = (key_gradient.astype(BF16), value_gradient.astype(BF16))
        for j, columns in enumerate((*both, k, v)):
            near_ref[rows, pl.ds(j * HEAD_WIDTH, HEAD_WIDTH)] = columns


def low_kernel(hidden_ref, down_ref, after_ref, out_ref):
    out_ref[...] = nt(down_ref[...], hidden_ref[...]).astype(BF16)


def grads_kernel(
    scale, state_ref, gq_ref, near_ref, d_ref, up_ref, kvup_ref, low_ref,
    query_ref, key_ref, value_ref, send_ref,
):
    tokens, width = d_ref.shape
    half = tokens // 2
    rank = low_ref.shape[0]
    size, state_rows, _ = state_ref.shape
    state_rows //= 2
    prefix, suffix = (
        jnp.concatenate(
            [state_ref[i, pl.ds(j * state_rows, state_rows), :] for i in range(size)], axis=0
        )
        for j in range(2)
    )
    backs = []
    for i in range(2):
        rows = pl.ds(i * half, half)
        local_k, local_v, k, v = (
            near_ref[rows, pl.ds(j * HEAD_WIDTH, HEAD_WIDTH)] for j in range(4)
        )
        key_gradient = (scale * (local_k.astype(F32) + nt(v, suffix))).astype(BF16)
        value_gradient = (scale * (local_v.astype(F32) + nn(k, suffix))).astype(BF16)
        key_ref[rows, :] = key_gradient
        value_ref[rows, :] = value_gradient
        back = jnp.zeros((ADAPTER_RANK, half), F32)
        for h in range(width // HEAD_WIDTH):
            at = pl.ds(h * HEAD_WIDTH, HEAD_WIDTH)
            grad_query = gq_ref[rows, at].astype(F32) + nt(d_ref[rows, at], prefix)
            grad_query = (scale * grad_query).astype(BF16)
            query_ref[rows, at] = grad_query
            back += nt(up_ref[:, at], grad_query)
        backs.append(
            jnp.concatenate(
                [
                    back,
                    nt(kvup_ref[pl.ds(0, ADAPTER_RANK), :], key_gradient),
                    nt(kvup_ref[pl.ds(ADAPTER_RANK, ADAPTER_RANK), :], value_gradient),
                ],
                axis=0,
            )
        )
    whole = jnp.concatenate(backs, axis=1).astype(BF16)
    for i in range(send_ref.shape[0]):
        send_ref[i, pl.ds(0, rank), :] = whole
        send_ref[i, pl.ds(rank, rank), :] = low_ref[...]


def down_kernel(parts_ref, hidden_ref, query_ref, key_ref, value_ref, out_ref):
    peers, rows, _ = parts_ref.shape
    rank = rows // 2
    heads = hidden_ref.shape[1] // HEAD_WIDTH
    both = sum(parts_ref[i].astype(F32) for i in range(peers)).astype(BF16)
    back, low = both[:rank], both[rank:]
    down = nn(back, hidden_ref[...]).astype(BF16)
    up_query = nn(low[:ADAPTER_RANK], query_ref[...]).astype(BF16)
    at = heads * rank
    for i in range(heads):
        part = slice(i * HEAD_WIDTH, (i + 1) * HEAD_WIDTH)
        out_ref[pl.ds(i * rank, rank), :] = down[:, part]
        out_ref[pl.ds(at + i * ADAPTER_RANK, ADAPTER_RANK), :] = up_query[:, part]
    at += heads * ADAPTER_RANK
    out_ref[pl.ds(at, ADAPTER_RANK), :] = nn(
        low[ADAPTER_RANK : 2 * ADAPTER_RANK], key_ref[...]
    ).astype(BF16)
    at += ADAPTER_RANK
    out_ref[pl.ds(at, ADAPTER_RANK), :] = nn(
        low[2 * ADAPTER_RANK :], value_ref[...]
    ).astype(BF16)
    at += ADAPTER_RANK
    out_ref[pl.ds(at, out_ref.shape[0] - at), :] = jnp.zeros(
        (out_ref.shape[0] - at, HEAD_WIDTH), BF16
    )


def sum_kernel(x_ref, out_ref):
    rows = x_ref.shape[0]
    row, column = grid2(16, rows)
    total = nn(ones_where(lax.rem(column, GRAD_ROWS) == row), x_ref[...]).astype(BF16)
    row, column = grid2(rows, 16)
    out_ref[...] = nn(ones_where(lax.rem(row, GRAD_ROWS) == column), total).astype(BF16)


def finish_kernel(scale, x_ref, down_ref, query_ref, kv_ref):
    rank = down_ref.shape[0]
    parts = down_ref.shape[1] // HEAD_WIDTH
    for i in range(parts):
        at = pl.ds(i * HEAD_WIDTH, HEAD_WIDTH)
        down_ref[:, at] = scale * x_ref[pl.ds(i * rank, rank), :].astype(F32)
    start = parts * rank
    for i in range(parts):
        at = pl.ds(i * HEAD_WIDTH, HEAD_WIDTH)
        query_ref[:, at] = scale * x_ref[
            pl.ds(start + i * ADAPTER_RANK, ADAPTER_RANK), :
        ].astype(F32)
    start += parts * ADAPTER_RANK
    kv_ref[...] = scale * x_ref[pl.ds(start, 2 * ADAPTER_RANK), :].astype(F32)


def shape(dims, dtype):
    return jax.ShapeDtypeStruct(dims, dtype)


def call(kernel, out_shape, flops, nbytes, name, mebibytes=16, **more):
    return pl.pallas_call(
        kernel,
        out_shape=out_shape,
        compiler_params=params(mebibytes),
        cost_estimate=pl.CostEstimate(flops=flops, bytes_accessed=nbytes, transcendentals=0),
        name=name,
        **more,
    )


def exchange(blocks, axis):
    return lax.all_to_all(blocks, axis, split_axis=0, concat_axis=0, tiled=True)


def on_device(hidden, query, key, value, d_out, down, up_query, kv_up):
    tokens, width = query.shape
    heads = width // HEAD_WIDTH
    ctx_axes = ("ring", "place")
    ctx, size, peers = (lax.axis_size(axis) for axis in (ctx_axes, "place", "head"))
    ranks = down.shape[0]
    att_scale = 1.0 / math.sqrt(HEAD_WIDTH * tokens * ctx)
    grad_scale = 1.0 / math.sqrt(tokens * ctx)
    state_rows = 2 * HEAD_WIDTH // size

    block = (tokens, HEAD_WIDTH)
    hbm = pl.BlockSpec(memory_space=pltpu.HBM)
    sent, chunk = pl.pallas_call(
        states_kernel,
        in_specs=[hbm] * 4,
        out_shape=[
            shape((size, state_rows, HEAD_WIDTH), BF16),
            shape((2 * HEAD_WIDTH, HEAD_WIDTH), BF16),
        ],
        scratch_shapes=[
            pltpu.VMEM((tokens, width), BF16),
            pltpu.VMEM((tokens, width), BF16),
            pltpu.VMEM(block, BF16),
            pltpu.VMEM(block, BF16),
            pltpu.SemaphoreType.DMA((6,)),
        ],
        compiler_params=params(ALONE),
        cost_estimate=pl.CostEstimate(
            flops=10**8, bytes_accessed=2 * 10**6, transcendentals=0
        ),
        name="states",
    )(query, d_out, key, value)
    ring_states = exchange(sent, "place")

    low = call(low_kernel, shape((ranks, tokens), BF16), 10**8, 2 * 10**6, "low")(
        hidden, down, chunk
    )

    ring_sums, chunk = call(
        ring_kernel,
        [shape((RINGS, state_rows // 2, HEAD_WIDTH), BF16), shape((2 * HEAD_WIDTH, HEAD_WIDTH), BF16)],
        10**6,
        2 * 10**5,
        "ring",
    )(ring_states, chunk, low)
    other_rings = exchange(ring_sums, "ring")
    local_q, near = call(
        local_kernel,
        [shape((tokens, width), BF16), shape((tokens, 4 * HEAD_WIDTH), BF16)],
        2 * 10**9,
        5 * 10**6,
        "local",
    )(query, d_out, key, value, chunk)
    scanned = call(
        scan_kernel,
        shape((size, state_rows, HEAD_WIDTH), BF16),
        10**6,
        2 * 10**5,
        "scan",
    )(ring_states, other_rings, near)
    around = exchange(scanned, "place")

    grad_query, key_gradient, value_gradient, copies = call(
        functools.partial(grads_kernel, att_scale),
        [
            shape((tokens, width), BF16),
            shape(block, BF16),
            shape(block, BF16),
            shape((peers, 2 * ranks, tokens), BF16),
        ],
        2 * 10**8,
        5 * 10**6,
        "grads",
    )(
        around, local_q, near, d_out, up_query, kv_up, low
    )
    both_parts = exchange(copies, "head")
    rows = ctx * GRAD_ROWS
    partial = call(down_kernel, shape((rows, HEAD_WIDTH), BF16), 5 * 10**7, 2 * 10**6, "down")(
        both_parts, hidden, grad_query, key_gradient, value_gradient
    )
    split = (ctx, GRAD_ROWS // 2, 2, HEAD_WIDTH)
    gathered = exchange(partial.reshape(split), ctx_axes)
    sums = call(sum_kernel, shape((rows, HEAD_WIDTH), BF16), 10**7, 3 * 10**5, "sum")(
        gathered.reshape(rows, HEAD_WIDTH)
    )
    result = exchange(sums.reshape(split), ctx_axes)
    grad_down, grad_up_query, grad_up_kv = call(
        functools.partial(finish_kernel, grad_scale),
        [
            shape((ranks, width), F32),
            shape((ADAPTER_RANK, width), F32),
            shape((2 * ADAPTER_RANK, HEAD_WIDTH), F32),
        ],
        10**6,
        5 * 10**5,
        "finish",
    )(result.reshape(rows, HEAD_WIDTH))
    return grad_query, key_gradient, value_gradient, grad_down, grad_up_query, grad_up_kv


def solution(mesh):
    ctx, peers = mesh.devices.shape
    by_ring = Mesh(
        mesh.devices.reshape(RINGS, ctx // RINGS, peers), ("ring", "place", "head")
    )
    both = P(("ring", "place"), "head")
    over_head = P(None, "head")
    return jax.shard_map(
        on_device,
        mesh=by_ring,
        in_specs=(both,) * 5 + (over_head,) * 3,
        out_specs=(both,) * 3 + (over_head,) * 3,
        check_vma=False,
    )
```
